32 devices in a mesh: dp: 8 (over z, x), tensor: 4 (over y, core).
Axes of the slice: x: 2, y: 2, z: 4, core: 2. Of those that a mesh axis runs over, the one named last changes fastest.
Arguments:
- hidden_in: bfloat16 [4, 4096, 1024], P(None, 'dp'), may hold values from -6 to 6
- cotangent: bfloat16 [4, 4096, 1024], P(None, 'dp'), may hold values from -6 to 6
- doc_lengths: int32 [4, 6], replicated, may hold values from 1 to 3584, as said below
- norm1_gain: float32 [1024], replicated, may hold values from 0.1 to 1.9
- norm1_bias: float32 [1024], replicated, may hold values from -1.75 to 1.75
- norm2_gain: float32 [1024], replicated, may hold values from 0.1 to 1.9
- norm2_bias: float32 [1024], replicated, may hold values from -1.75 to 1.75
- qkv_weight: bfloat16 [1024, 16, 192], P('dp', 'tensor'), may hold values from -0.1875 to 0.1875
- qkv_bias: float32 [16, 192], P('tensor'), may hold values from -1.75 to 1.75
- out_weight: bfloat16 [16, 64, 1024], P('tensor', None, 'dp'), may hold values from -1 to 1
- out_bias: float32 [1024], replicated, may hold values from -3 to 3
- fc1_weight: bfloat16 [1024, 4096], P('dp', 'tensor'), may hold values from -0.1875 to 0.1875
- fc1_bias: float32 [4096], P('tensor'), may hold values from -3 to 3
- fc2_weight: bfloat16 [4096, 1024], P('tensor', 'dp'), may hold values from -0.09375 to 0.09375
Outputs:
- layer_out: bfloat16 [4, 4096, 1024], P(None, 'dp')
- grad_input: bfloat16 [4, 4096, 1024], P(None, 'dp')
- grad_norm1_gain: float32 [1024], replicated
- grad_norm1_bias: float32 [1024], replicated
- grad_norm2_gain: float32 [1024], replicated
- grad_norm2_bias: float32 [1024], replicated
- grad_qkv_weight: float32 [1024, 16, 192], P('dp', 'tensor')
- grad_qkv_bias: float32 [16, 192], P('tensor')
- grad_out_weight: float32 [16, 64, 1024], P('tensor', None, 'dp')
- grad_out_bias: float32 [1024], replicated
- grad_fc1_weight: float32 [1024, 4096], P('dp', 'tensor')
- grad_fc1_bias: float32 [4096], P('tensor')
- grad_fc2_weight: float32 [4096, 1024], P('tensor', 'dp')
The draws below stay inside these ranges and needn't reach their ends.
Inputs may be any that keep to these rules, and one draw needn't show every extreme that they name: `doc_lengths`: each row lists the lengths of the 6 documents packed in order into one sequence; each row sums to 4096. In every row but one, each document has 200 to min(2000, 3584) tokens; in one row, drawn from the seed, one document has exactly 3584 tokens and the others are short.
All inputs are finite; a program needn't handle non-finite values.
Results may differ from the reference program's by a relative error of at most 0.015.
Values may be sent and summed in bfloat16 or wider, within the bound.
A program may use at most 192 MiB of HBM per device.

```python
from functools import partial
import jax
import jax.numpy as jnp
from jax import lax

D = 1024
HEADS = 16
HEAD = 64
ROT = 16
FF = 4096
TOK_DEV = 512
MICRO = 4
DOC_MIN = 200
DOC_MAX = 2000
LENGTH = 4096
DOCS = 6


def pieces_of(cuts, total):
    bounds = jnp.concatenate([jnp.zeros((1,), jnp.int32), jnp.sort(cuts).astype(jnp.int32), jnp.reshape(total, (1,)).astype(jnp.int32)])
    return bounds[1:] - bounds[:-1]


def refill(extras, room_cap, total):
    capped = jnp.minimum(extras, room_cap)
    remaining = total - jnp.sum(capped)
    room = room_cap - capped
    before = jnp.cumsum(room) - room
    return capped + jnp.clip(remaining - before, 0, room)


def spread_row(each_key):
    spare = LENGTH - DOCS * DOC_MIN
    room_cap = min(DOC_MAX, LENGTH - TOK_DEV) - DOC_MIN
    cuts = jax.random.randint(each_key, (DOCS - 1,), 0, spare + 1)
    extras = pieces_of(cuts, spare)
    return (DOC_MIN + refill(extras, room_cap, spare)).astype(jnp.int32)


def draw_doc_lengths(key, part):
    key = jax.random.fold_in(key, 7)
    pick_key, spread_key, head_key, tail_key = jax.random.split(key, 4)
    chosen = jax.random.randint(pick_key, (), 0, MICRO)
    spread = jax.vmap(spread_row)(jax.random.split(spread_key, MICRO))
    head_len = jax.random.randint(head_key, (), 1, TOK_DEV - DOCS + 3).astype(jnp.int32)
    tail_spare = TOK_DEV - head_len - (DOCS - 2)
    tail_cuts = jax.random.randint(tail_key, (DOCS - 3,), 0, tail_spare + 1)
    tail = 1 + pieces_of(tail_cuts, tail_spare)
    long_row = jnp.concatenate([jnp.reshape(head_len, (1,)), jnp.full((1,), LENGTH - TOK_DEV, jnp.int32), tail.astype(jnp.int32)])
    return jnp.where((jnp.arange(MICRO) == chosen)[:, None], long_row[None, :], spread).astype(jnp.int32)


def steps_of(stream_key, extent, cuts, smallest, largest):
    def one(dim, parts):
        heights = jax.random.uniform(jax.random.fold_in(jax.random.fold_in(stream_key, 6), dim), (parts,), jnp.float32, smallest / len(cuts), largest / len(cuts))
        return jnp.repeat(jnp.exp(heights), extent[dim] // parts).reshape((-1,) + (1,) * (len(extent) - dim - 1))

    factor_of = one(*cuts[0])
    for cut in cuts[1:]:
        factor_of = factor_of * one(*cut)
    return factor_of


def normal_values(key, dims, width, most, pieces=(), held_as=jnp.bfloat16):
    level = steps_of(key, dims, pieces, -0.22, 0.18) if pieces else 1.0
    result = jax.random.normal(key, dims, jnp.float32) * width * level
    return jnp.minimum(jnp.maximum(result, -most), most).astype(held_as)


def setup_inputs(seed: int = 0) -> dict:
    splits = jax.random.split(jax.random.key(seed), 15)
    hidden_in = normal_values(splits[0], (MICRO, LENGTH, D), 1.0, 6.0, ((1, 8),))
    cotangent = normal_values(splits[1], (MICRO, LENGTH, D), 1.0, 6.0, ((1, 8),))
    doc_lengths = draw_doc_lengths(jax.random.fold_in(splits[14], 71), 0)
    norm1_gain = jnp.clip(1.0 + 0.18 * jax.random.normal(splits[3], (D,), jnp.float32), 0.1, 1.9)
    norm1_bias = normal_values(splits[4], (D,), 0.3, 1.75, (), jnp.float32)
    norm2_gain = jnp.clip(1.0 + 0.18 * jax.random.normal(splits[5], (D,), jnp.float32), 0.1, 1.9)
    norm2_bias = normal_values(splits[6], (D,), 0.3, 1.75, (), jnp.float32)
    qkv_weight = normal_values(splits[7], (D, HEADS, 3 * HEAD), D ** -0.5, 0.1875, ((0, 8), (1, 4)))
    qkv_bias = normal_values(splits[8], (HEADS, 3 * HEAD), 0.3, 1.75, ((0, 4),), jnp.float32)
    out_weight = normal_values(splits[9], (HEADS, HEAD, D), (HEADS * HEAD // 32) ** -0.5, 1.0, ((0, 4), (2, 8)))
    out_bias = normal_values(splits[10], (D,), 0.5, 3.0, (), jnp.float32)
    fc1_weight = normal_values(splits[11], (D, FF), D ** -0.5, 0.1875, ((0, 8), (1, 4)))
    fc1_bias = normal_values(splits[12], (FF,), 0.5, 3.0, ((0, 4),), jnp.float32)
    fc2_weight = normal_values(splits[13], (FF, D), FF ** -0.5, 0.09375, ((0, 4), (1, 8)))
    return dict(hidden_in=hidden_in, cotangent=cotangent, doc_lengths=doc_lengths, norm1_gain=norm1_gain, norm1_bias=norm1_bias, norm2_gain=norm2_gain, norm2_bias=norm2_bias, qkv_weight=qkv_weight, qkv_bias=qkv_bias, out_weight=out_weight, out_bias=out_bias, fc1_weight=fc1_weight, fc1_bias=fc1_bias, fc2_weight=fc2_weight)


norm_epsilon = 1e-05
masked_score = -1e+30

@jax.custom_vjp
def low(v):
    return lax.optimization_barrier(v.astype(jnp.bfloat16)).astype(jnp.float32)

@jax.custom_vjp
def low_back(v):
    return v

def low_keep(v):
    return (low(v), None)

def low_pass(kept, grad):
    return (grad,)

def back_keep(v):
    return (v, None)

def back_low(kept, grad):
    return (low(grad),)
low.defvjp(low_keep, low_pass)
low_back.defvjp(back_keep, back_low)

def documents(lengths, token_index):
    bounds = jnp.cumsum(lengths).astype(jnp.int32)
    passed = bounds[None, :] <= token_index[:, None]
    segment = lax.optimization_barrier(jnp.sum(passed.astype(jnp.int32), axis=1))
    doc_start = lax.optimization_barrier(jnp.max(jnp.where(passed, bounds[None, :], 0), axis=1))
    return (segment, token_index - doc_start)

def rotary_angles(position):
    half_width = ROT // 2
    frequency = jnp.power(10000.0, -2.0 * jnp.arange(half_width, dtype=jnp.float32) / ROT)
    angles = position.astype(jnp.float32)[..., None] * frequency
    return (jnp.cos(angles)[..., None, :], jnp.sin(angles)[..., None, :])

def rotary(vectors, cosine_table, sine_table):
    half_width = cosine_table.shape[-1]
    lower_half = vectors[..., :half_width]
    upper_half = vectors[..., half_width:2 * half_width]
    return jnp.concatenate([lower_half * cosine_table - upper_half * sine_table, upper_half * cosine_table + lower_half * sine_table, vectors[..., 2 * half_width:]], axis=-1)

def layer_norm(values, gain, bias):
    centered = values - lax.optimization_barrier(jnp.mean(values, axis=-1, keepdims=True))
    variance = lax.optimization_barrier(jnp.mean(centered * centered, axis=-1, keepdims=True))
    return centered * lax.rsqrt(variance + norm_epsilon) * gain + bias

def head_attention(segment, inputs):
    queries, keys_rot, values = inputs
    token_index = jnp.arange(LENGTH, dtype=jnp.int32)
    scores = low_back(jnp.dot(queries, keys_rot.T, precision=lax.Precision.HIGHEST) * HEAD ** (-0.5))
    allowed = (token_index[:, None] >= token_index[None, :]) & (segment[:, None] == segment[None, :])
    masked = jnp.where(allowed, scores, masked_score)
    top_score = lax.optimization_barrier(jnp.max(masked, axis=-1, keepdims=True))
    exponent = jnp.where(allowed, jnp.exp(masked - top_score), 0.0)
    attn_probs = exponent / lax.optimization_barrier(jnp.sum(exponent, axis=-1, keepdims=True))
    return jnp.dot(low(attn_probs), values, precision=lax.Precision.HIGHEST)

def sequence_attention(inputs):
    seq_queries, seq_keys, seq_values, segment = inputs
    return lax.map(jax.checkpoint(partial(head_attention, segment)), (seq_queries, seq_keys, seq_values))

def reference(hidden_in, cotangent, doc_lengths, norm1_gain, norm1_bias, norm2_gain, norm2_bias, qkv_weight, qkv_bias, out_weight, out_bias, fc1_weight, fc1_bias, fc2_weight):
    token_index = jnp.arange(LENGTH, dtype=jnp.int32)
    segment, position = jax.vmap(partial(documents, token_index=token_index))(doc_lengths)
    cosine_table, sine_table = rotary_angles(position)
    highest = lax.Precision.HIGHEST

    def forward(parameters, hidden):
        gain_one, bias_one, gain_two, bias_two, w_qkv, b_qkv, w_out, b_out, w_up, b_up, w_down = parameters
        first_norm = low(layer_norm(hidden, gain_one, bias_one))
        second_norm = low(layer_norm(hidden, gain_two, bias_two))
        projected = low_back(jnp.einsum('mtd,dhe->mthe', first_norm, w_qkv, precision=highest) + b_qkv)
        queries = low(rotary(projected[..., :HEAD], cosine_table, sine_table))
        keys_rot = low(rotary(projected[..., HEAD:2 * HEAD], cosine_table, sine_table))
        values = low(projected[..., 2 * HEAD:])
        attended = lax.map(sequence_attention, (jnp.swapaxes(queries, 1, 2), jnp.swapaxes(keys_rot, 1, 2), jnp.swapaxes(values, 1, 2), segment))
        attended = low(low_back(attended))
        attn_out = jnp.einsum('mhte,hed->mtd', attended, w_out, precision=highest)
        up_proj = low_back(jnp.einsum('mtd,df->mtf', second_norm, w_up, precision=highest) + b_up)
        act_low = low(jax.nn.gelu(up_proj, approximate=False))
        down = jnp.einsum('mtf,fd->mtd', act_low, w_down, precision=highest)
        return hidden + low_back(attn_out + down) + b_out
    parameters = (norm1_gain.astype(jnp.float32), norm1_bias.astype(jnp.float32), norm2_gain.astype(jnp.float32), norm2_bias.astype(jnp.float32), qkv_weight.astype(jnp.float32), qkv_bias.astype(jnp.float32), out_weight.astype(jnp.float32), out_bias.astype(jnp.float32), fc1_weight.astype(jnp.float32), fc1_bias.astype(jnp.float32), fc2_weight.astype(jnp.float32))
    output, pullback = jax.vjp(forward, parameters, hidden_in.astype(jnp.float32))
    grad_params, grad_hidden = pullback(cotangent.astype(jnp.float32))
    return (output.astype(jnp.bfloat16), grad_hidden.astype(jnp.bfloat16), grad_params[0], grad_params[1], grad_params[2], grad_params[3], grad_params[4], grad_params[5], grad_params[6], grad_params[7], grad_params[8], grad_params[9], grad_params[10])
```

```python
from functools import partial
import math

import jax
import jax.numpy as jnp
from jax import lax
from jax.experimental import pallas as pl
from jax.experimental.pallas import tpu as pltpu
from jax.sharding import PartitionSpec as P

HEAD = 64
ROT = 16


norm_epsilon = 1e-05
masked_score = -1e30


def documents(lengths, token_index):
    bounds = jnp.cumsum(lengths)
    passed = bounds[None, :] <= token_index[:, None]
    segment = jnp.sum(passed.astype(jnp.int32), axis=1)
    doc_start = jnp.max(jnp.where(passed, bounds[None, :], 0), axis=1)
    return (segment, token_index - doc_start)


def rotary_angles(position):
    half_width = ROT // 2
    frequency = jnp.power(10000.0, -2.0 * jnp.arange(half_width, dtype=jnp.float32) / ROT)
    angles = position.astype(jnp.float32)[..., None] * frequency
    return (jnp.cos(angles)[..., None, :], jnp.sin(angles)[..., None, :])


def rotary(vectors, cosine_table, sine_table):
    half_width = cosine_table.shape[-1]
    lower_half = vectors[..., :half_width]
    upper_half = vectors[..., half_width : 2 * half_width]
    return jnp.concatenate(
        [
            lower_half * cosine_table - upper_half * sine_table,
            upper_half * cosine_table + lower_half * sine_table,
            vectors[..., 2 * half_width :],
        ],
        axis=-1,
    )


NT = (((1,), (1,)), ((), ()))
TN = (((0,), (0,)), ((), ()))
NN = (((1,), (0,)), ((), ()))
score_scale = HEAD**-0.5
vmem_bytes = 44 * 1024 * 1024


def mul(a, b, dims):
    return lax.dot_general(a, b, dims, preferred_element_type=jnp.float32)


def attend_kernel(rows, first_ref, x_ref, start_ref, out_ref, lse_ref, delta_ref):
    unit, block = pl.program_id(0), pl.program_id(1)
    own = x_ref[0, pl.ds(pl.multiple_of(block * rows, rows), rows), :]
    queries = own[:, :HEAD] * jnp.bfloat16(score_scale)
    grad_att = own[:, 3 * HEAD :]
    query_index = block * rows + lax.broadcasted_iota(jnp.int32, (1, rows), 1)
    start = start_ref[0]

    def step(key_block, carry):
        top, total, acc = carry
        piece = x_ref[0, pl.ds(pl.multiple_of(key_block * rows, rows), rows), :]
        scores = mul(piece[:, HEAD : 2 * HEAD], queries, NT)
        key_index = key_block * rows + lax.broadcasted_iota(jnp.int32, (rows, rows), 0)
        allowed = (key_index <= query_index) & (key_index >= start)
        scores = jnp.where(allowed, scores, masked_score)
        new_top = jnp.maximum(top, jnp.max(scores, axis=0, keepdims=True))
        decay = jnp.exp(top - new_top)
        exponent = jnp.exp(scores - new_top)
        total = total * decay + jnp.sum(exponent, axis=0, keepdims=True)
        acc = acc * decay + mul(
            piece[:, 2 * HEAD : 3 * HEAD], exponent.astype(jnp.bfloat16), TN
        )
        return (new_top, total, acc)

    top, total, acc = lax.fori_loop(
        first_ref[unit, block],
        block + 1,
        step,
        (
            jnp.full((1, rows), masked_score, jnp.float32),
            jnp.zeros((1, rows), jnp.float32),
            jnp.zeros((HEAD, rows), jnp.float32),
        ),
    )
    attended = acc / total
    lse_ref[0] = top + jnp.log(total)
    delta_ref[0] = jnp.sum(attended * grad_att.astype(jnp.float32).T, axis=0, keepdims=True)
    out_ref[0] = attended.T.astype(jnp.bfloat16)


def attend_back_kernel(rows, last_ref, x_ref, start_ref, lse_ref, delta_ref, grad_ref, grad_q):
    unit, block = pl.program_id(0), pl.program_id(1)
    here = pl.ds(pl.multiple_of(block * rows, rows), rows)
    own = x_ref[0, here, :]
    keys, values = own[:, HEAD : 2 * HEAD], own[:, 2 * HEAD : 3 * HEAD]
    key_index = block * rows + lax.broadcasted_iota(jnp.int32, (rows, rows), 0)

    @pl.when(block == 0)
    def _():
        grad_q[...] = jnp.zeros_like(grad_q)

    def step(query_block, carry):
        grad_keys, grad_values = carry
        there = pl.ds(pl.multiple_of(query_block * rows, rows), rows)
        piece = x_ref[0, there, :]
        queries = piece[:, :HEAD] * jnp.bfloat16(score_scale)
        grad_att = piece[:, 3 * HEAD :]
        query_index = query_block * rows + lax.broadcasted_iota(jnp.int32, (1, rows), 1)
        allowed = (key_index <= query_index) & (key_index >= start_ref[0, :, there])
        scores = mul(keys, queries, NT)
        probs = jnp.where(allowed, jnp.exp(scores - lse_ref[0, :, there]), 0.0)
        grad_values = grad_values + mul(probs.astype(jnp.bfloat16), grad_att, NN)
        grad_probs = mul(values, grad_att, NT)
        grad_scores = (probs * (grad_probs - delta_ref[0, :, there])).astype(jnp.bfloat16)
        grad_keys = grad_keys + mul(grad_scores, queries, NN)
        grad_q[there, :] += mul(grad_scores, keys, TN)
        return (grad_keys, grad_values)

    zero = jnp.zeros((rows, HEAD), jnp.float32)
    grad_keys, grad_values = lax.fori_loop(block, last_ref[unit, block] + 1, step, (zero, zero))
    grad_ref[0, here, HEAD : 2 * HEAD] = grad_keys.astype(jnp.bfloat16)
    grad_ref[0, here, 2 * HEAD :] = grad_values.astype(jnp.bfloat16)

    @pl.when(block == pl.num_programs(1) - 1)
    def _():
        grad_ref[0, :, :HEAD] = (grad_q[...] * score_scale).astype(jnp.bfloat16)


def attention(packed, lengths):
    units, length, width = packed.shape
    rows = math.gcd(length, 512)
    blocks = length // rows
    bounds = jnp.cumsum(lengths, axis=1)[:, None, :]
    token = jnp.arange(length, dtype=jnp.int32)[None, :, None]
    start = jnp.max(jnp.where(bounds <= token, bounds, 0), axis=2)
    end = jnp.min(jnp.where(bounds > token, bounds, length), axis=2)
    first = start[:, ::rows] // rows
    last = (end[:, rows - 1 :: rows] - 1) // rows
    start = start[:, None, :]
    whole = pl.BlockSpec((1, length, width), lambda u, b, s: (u, 0, 0))
    line = pl.BlockSpec((1, 1, rows), lambda u, b, s: (u, 0, b))
    full_line = pl.BlockSpec((1, 1, length), lambda u, b, s: (u, 0, 0))
    pairs = units * length * length // 4
    out, lse, delta = pl.pallas_call(
        partial(attend_kernel, rows),
        grid_spec=pltpu.PrefetchScalarGridSpec(
            num_scalar_prefetch=1,
            grid=(units, blocks),
            in_specs=[whole, line],
            out_specs=[pl.BlockSpec((1, rows, HEAD), lambda u, b, s: (u, b, 0)), line, line],
        ),
        out_shape=[
            jax.ShapeDtypeStruct((units, length, HEAD), jnp.bfloat16),
            jax.ShapeDtypeStruct((units, 1, length), jnp.float32),
            jax.ShapeDtypeStruct((units, 1, length), jnp.float32),
        ],
        compiler_params=pltpu.CompilerParams(vmem_limit_bytes=vmem_bytes),
        cost_estimate=pl.CostEstimate(
            flops=pairs * 4 * 256, bytes_accessed=units * length * 700, transcendentals=pairs
        ),
    )(first, packed, start)
    grads = pl.pallas_call(
        partial(attend_back_kernel, rows),
        grid_spec=pltpu.PrefetchScalarGridSpec(
            num_scalar_prefetch=1,
            grid=(units, blocks),
            in_specs=[whole, full_line, full_line, full_line],
            out_specs=pl.BlockSpec((1, length, 3 * HEAD), lambda u, b, s: (u, 0, 0)),
            scratch_shapes=[pltpu.VMEM((length, HEAD), jnp.float32)],
        ),
        out_shape=jax.ShapeDtypeStruct((units, length, 3 * HEAD), jnp.bfloat16),
        compiler_params=pltpu.CompilerParams(vmem_limit_bytes=vmem_bytes),
        cost_estimate=pl.CostEstimate(
            flops=pairs * 10 * 256, bytes_accessed=units * length * 1000, transcendentals=pairs
        ),
    )(last, packed, start, lse, delta)
    return (out, grads)


def shards(
    hidden_in,
    cotangent,
    doc_lengths,
    norm1_gain,
    norm1_bias,
    norm2_gain,
    norm2_bias,
    qkv_weight,
    qkv_bias,
    out_weight,
    out_bias,
    fc1_weight,
    fc1_bias,
    fc2_weight,
):
    micros, tok_rows, width = hidden_in.shape
    heads = qkv_bias.shape[0]
    hidden_units = fc1_bias.shape[0]
    shard_rows = qkv_weight.shape[0]
    dp_count = lax.axis_size("dp")
    tokens = micros * tok_rows
    qkv_wide, att_wide = heads * 3 * HEAD, heads * HEAD
    unit_count = micros * heads
    units = -(-unit_count // dp_count)

    att_weights = lax.all_gather(
        jnp.concatenate(
            [qkv_weight.reshape(shard_rows, qkv_wide), out_weight.reshape(att_wide, shard_rows).T],
            axis=1,
        ),
        "dp",
        axis=0,
        tiled=True,
    )
    w_qkv, w_out = att_weights[:, :qkv_wide], att_weights[:, qkv_wide:]
    ff_weights = lax.all_gather(
        jnp.concatenate([fc1_weight, fc2_weight.T], axis=1), "dp", axis=0, tiled=True
    )
    w_up, w_down = ff_weights[:, :hidden_units], ff_weights[:, hidden_units:]

    query_index = lax.axis_index("dp") * tok_rows + jnp.arange(tok_rows, dtype=jnp.int32)
    position = jax.vmap(lambda lengths: documents(lengths, query_index)[1])(doc_lengths)
    cosine_table, sine_table = rotary_angles(position.reshape(tokens))
    hidden = hidden_in.reshape(tokens, width).astype(jnp.float32)
    grad_low = cotangent.reshape(tokens, width)
    centered = hidden - jnp.mean(hidden, axis=-1, keepdims=True)
    variance = jnp.mean(centered * centered, axis=-1, keepdims=True)
    inverse = lax.rsqrt(variance + norm_epsilon)
    unit_norm = centered * inverse
    first_low = (unit_norm * norm1_gain + norm1_bias).astype(jnp.bfloat16)
    second_low = (unit_norm * norm2_gain + norm2_bias).astype(jnp.bfloat16)

    def to_units(array):
        wide = array.shape[-1]
        array = array.reshape(micros, tok_rows, heads, wide).transpose(2, 0, 1, 3)
        array = array.reshape(unit_count, tok_rows, wide)
        array = jnp.pad(array, ((0, units * dp_count - unit_count), (0, 0), (0, 0)))
        return lax.all_to_all(array, "dp", split_axis=0, concat_axis=1, tiled=True)

    def from_units(array):
        wide = array.shape[-1]
        array = lax.all_to_all(array, "dp", split_axis=1, concat_axis=0, tiled=True)
        array = array[:unit_count].reshape(heads, micros, tok_rows, wide)
        return array.transpose(1, 2, 0, 3).reshape(tokens, heads, wide)

    projected = (mul(first_low, w_qkv, NN) + qkv_bias.reshape(qkv_wide)).reshape(
        tokens, heads, 3 * HEAD
    )
    grad_att = mul(grad_low, w_out, NN).astype(jnp.bfloat16).reshape(tokens, heads, HEAD)
    packed = to_units(
        jnp.concatenate(
            [
                rotary(projected[..., :HEAD], cosine_table, sine_table).astype(jnp.bfloat16),
                rotary(projected[..., HEAD : 2 * HEAD], cosine_table, sine_table).astype(
                    jnp.bfloat16
                ),
                projected[..., 2 * HEAD :].astype(jnp.bfloat16),
                grad_att,
            ],
            axis=-1,
        )
    )
    unit_ids = lax.axis_index("dp") * units + jnp.arange(units, dtype=jnp.int32)
    unit_out, unit_grads = attention(packed, doc_lengths[unit_ids % micros])
    attended = from_units(unit_out).reshape(tokens, att_wide)
    grad_parts = from_units(unit_grads)

    up_proj = mul(second_low, w_up, NN) + fc1_bias
    activated, gelu_pull = jax.vjp(partial(jax.nn.gelu, approximate=False), up_proj)
    act_low = activated.astype(jnp.bfloat16)
    grad_up = gelu_pull(mul(grad_low, w_down, NN))[0].astype(jnp.bfloat16)
    grad_second = mul(grad_up, w_up, NT)
    branches = lax.psum(
        (mul(attended, w_out, NT) + mul(act_low, w_down, NT)).astype(jnp.bfloat16), "tensor"
    )
    layer_out = (hidden + branches.astype(jnp.float32) + out_bias).astype(jnp.bfloat16)

    early = lax.psum_scatter(
        jnp.concatenate(
            [
                mul(second_low, grad_up, TN).astype(jnp.bfloat16),
                mul(grad_low, act_low, TN).astype(jnp.bfloat16),
                mul(grad_low, attended, TN).astype(jnp.bfloat16),
            ],
            axis=1,
        ),
        "dp",
        scatter_dimension=0,
        tiled=True,
    ).astype(jnp.float32)
    grad_proj = jnp.concatenate(
        [
            rotary(grad_parts[..., :HEAD].astype(jnp.float32), cosine_table, -sine_table),
            rotary(
                grad_parts[..., HEAD : 2 * HEAD].astype(jnp.float32), cosine_table, -sine_table
            ),
            grad_parts[..., 2 * HEAD :].astype(jnp.float32),
        ],
        axis=-1,
    ).astype(jnp.bfloat16)
    grad_proj = grad_proj.reshape(tokens, qkv_wide)
    grad_first = mul(grad_proj, w_qkv, NT)
    grad_unit = (grad_first * norm1_gain + grad_second * norm2_gain).astype(jnp.bfloat16)
    grad_unit, branches_done = lax.optimization_barrier((grad_unit, layer_out))
    grad_unit = lax.psum(grad_unit, "tensor").astype(jnp.float32)
    late = lax.psum_scatter(
        mul(first_low, grad_proj, TN).astype(jnp.bfloat16), "dp", scatter_dimension=0, tiled=True
    ).astype(jnp.float32)
    grad_input = grad_low.astype(jnp.float32) + inverse * (
        grad_unit
        - jnp.mean(grad_unit, axis=-1, keepdims=True)
        - unit_norm * jnp.mean(grad_unit * unit_norm, axis=-1, keepdims=True)
    )
    norm_sums = lax.psum(
        jnp.stack(
            [
                jnp.sum(grad_first * unit_norm, axis=0),
                jnp.sum(grad_first, axis=0),
                jnp.sum(grad_second * unit_norm, axis=0),
                jnp.sum(grad_second, axis=0),
            ]
        ),
        ("dp", "tensor"),
    )
    grad_b_qkv, grad_b_up, grad_b_out = lax.psum(
        (
            jnp.sum(grad_proj.astype(jnp.float32), axis=0),
            jnp.sum(grad_up.astype(jnp.float32), axis=0),
            jnp.sum(grad_low.astype(jnp.float32), axis=0),
        ),
        "dp",
    )
    return (
        branches_done.reshape(hidden_in.shape),
        grad_input.astype(jnp.bfloat16).reshape(hidden_in.shape),
        norm_sums[0],
        norm_sums[1],
        norm_sums[2],
        norm_sums[3],
        late.reshape(shard_rows, heads, 3 * HEAD),
        grad_b_qkv.reshape(heads, 3 * HEAD),
        early[:, 2 * hidden_units :].T.reshape(heads, HEAD, shard_rows),
        grad_b_out,
        early[:, :hidden_units],
        grad_b_up,
        early[:, hidden_units : 2 * hidden_units].T,
    )


def solution(mesh):
    return jax.shard_map(
        shards,
        mesh=mesh,
        in_specs=(
            P(None, "dp", None),
            P(None, "dp", None),
            P(),
            P(),
            P(),
            P(),
            P(),
            P("dp", "tensor", None),
            P("tensor", None),
            P("tensor", None, "dp"),
            P(),
            P("dp", "tensor"),
            P("tensor"),
            P("tensor", "dp"),
        ),
        out_specs=(
            P(None, "dp", None),
            P(None, "dp", None),
            P(),
            P(),
            P(),
            P(),
            P("dp", "tensor", None),
            P("tensor", None),
            P("tensor", None, "dp"),
            P(),
            P("dp", "tensor"),
            P("tensor"),
            P("tensor", "dp"),
        ),
        check_vma=False,
    )
```

```python
from functools import partial
import math

import jax
import jax.numpy as jnp
from jax import lax
from jax.experimental import pallas as pl
from jax.experimental.pallas import tpu as pltpu
from jax.sharding import PartitionSpec as P

HEAD = 64
ROT = 16


norm_epsilon = 1e-05
masked_score = -1e30


def documents(lengths, token_index):
    bounds = jnp.cumsum(lengths)
    passed = bounds[None, :] <= token_index[:, None]
    segment = jnp.sum(passed.astype(jnp.int32), axis=1)
    doc_start = jnp.max(jnp.where(passed, bounds[None, :], 0), axis=1)
    return (segment, token_index - doc_start)


def rotary_angles(position):
    half_width = ROT // 2
    frequency = jnp.power(10000.0, -2.0 * jnp.arange(half_width, dtype=jnp.float32) / ROT)
    angles = position.astype(jnp.float32)[..., None] * frequency
    return (jnp.cos(angles)[..., None, :], jnp.sin(angles)[..., None, :])


def rotary(vectors, cosine_table, sine_table):
    half_width = cosine_table.shape[-1]
    lower_half = vectors[..., :half_width]
    upper_half = vectors[..., half_width : 2 * half_width]
    return jnp.concatenate(
        [
            lower_half * cosine_table - upper_half * sine_table,
            upper_half * cosine_table + lower_half * sine_table,
            vectors[..., 2 * half_width :],
        ],
        axis=-1,
    )


NT = (((1,), (1,)), ((), ()))
TN = (((0,), (0,)), ((), ()))
NN = (((1,), (0,)), ((), ()))
score_scale = HEAD**-0.5
vmem_bytes = 44 * 1024 * 1024


def mul(a, b, dims):
    return lax.dot_general(a, b, dims, preferred_element_type=jnp.float32)


def attend_kernel(units, first_ref, x_ref, start_ref, out_ref, lse_ref, delta_ref):
    block = pl.program_id(0)
    rows = x_ref.shape[1]
    query_index = block * rows + lax.broadcasted_iota(jnp.int32, (1, rows), 1)
    for unit in range(units):
        base = unit * 4 * HEAD
        own = x_ref[block, :, base : base + 4 * HEAD]
        queries = own[:, :HEAD] * jnp.bfloat16(score_scale)
        grad_att = own[:, 3 * HEAD :]
        start = start_ref[unit]

        def step(key_block, carry):
            top, total, acc = carry
            piece = x_ref[key_block, :, base : base + 4 * HEAD]
            scores = mul(piece[:, HEAD : 2 * HEAD], queries, NT)
            key_index = key_block * rows + lax.broadcasted_iota(jnp.int32, (rows, rows), 0)
            allowed = (key_index <= query_index) & (key_index >= start)
            scores = jnp.where(allowed, scores, masked_score)
            new_top = jnp.maximum(top, jnp.max(scores, axis=0, keepdims=True))
            decay = jnp.exp(top - new_top)
            exponent = jnp.exp(scores - new_top)
            total = total * decay + jnp.sum(exponent, axis=0, keepdims=True)
            acc = acc * decay + mul(
                piece[:, 2 * HEAD : 3 * HEAD], exponent.astype(jnp.bfloat16), TN
            )
            return (new_top, total, acc)

        top, total, acc = lax.fori_loop(
            first_ref[unit, block],
            block + 1,
            step,
            (
                jnp.full((1, rows), masked_score, jnp.float32),
                jnp.zeros((1, rows), jnp.float32),
                jnp.zeros((HEAD, rows), jnp.float32),
            ),
        )
        attended = acc / total
        lse_ref[unit] = top + jnp.log(total)
        delta_ref[unit] = jnp.sum(attended * grad_att.astype(jnp.float32).T, axis=0, keepdims=True)
        out_ref[0, :, unit * HEAD : (unit + 1) * HEAD] = attended.T.astype(jnp.bfloat16)


def attend_back_kernel(units, last_ref, x_ref, start_ref, lse_ref, delta_ref, grad_ref, grad_q):
    block = pl.program_id(0)
    rows = x_ref.shape[1]
    key_index = block * rows + lax.broadcasted_iota(jnp.int32, (rows, rows), 0)

    @pl.when(block == 0)
    def _():
        grad_q[...] = jnp.zeros_like(grad_q)

    for unit in range(units):
        base = unit * 4 * HEAD
        own = x_ref[block, :, base : base + 4 * HEAD]
        keys, values = own[:, HEAD : 2 * HEAD], own[:, 2 * HEAD : 3 * HEAD]

        def step(query_block, carry):
            grad_keys, grad_values = carry
            there = pl.ds(pl.multiple_of(query_block * rows, rows), rows)
            piece = x_ref[query_block, :, base : base + 4 * HEAD]
            queries = piece[:, :HEAD] * jnp.bfloat16(score_scale)
            grad_att = piece[:, 3 * HEAD :]
            query_index = query_block * rows + lax.broadcasted_iota(jnp.int32, (1, rows), 1)
            allowed = (key_index <= query_index) & (key_index >= start_ref[unit, :, there])
            scores = mul(keys, queries, NT)
            probs = jnp.where(allowed, jnp.exp(scores - lse_ref[unit, :, there]), 0.0)
            grad_values = grad_values + mul(probs.astype(jnp.bfloat16), grad_att, NN)
            grad_probs = mul(values, grad_att, NT)
            grad_scores = (probs * (grad_probs - delta_ref[unit, :, there])).astype(jnp.bfloat16)
            grad_keys = grad_keys + mul(grad_scores, queries, NN)
            grad_q[unit, query_block] += mul(grad_scores, keys, TN)
            return (grad_keys, grad_values)

        zero = jnp.zeros((rows, HEAD), jnp.float32)
        grad_keys, grad_values = lax.fori_loop(
            block, last_ref[unit, block] + 1, step, (zero, zero)
        )
        base = unit * 3 * HEAD
        grad_ref[0, :, base : base + HEAD] = (grad_q[unit, block] * score_scale).astype(
            jnp.bfloat16
        )
        grad_ref[0, :, base + HEAD : base + 2 * HEAD] = grad_keys.astype(jnp.bfloat16)
        grad_ref[0, :, base + 2 * HEAD : base + 3 * HEAD] = grad_values.astype(jnp.bfloat16)


def attention(packed, lengths):
    blocks, rows, width = packed.shape
    units = width // (4 * HEAD)
    length = blocks * rows
    bounds = jnp.cumsum(lengths, axis=1)[:, None, :]
    token = jnp.arange(length, dtype=jnp.int32)[None, :, None]
    start = jnp.max(jnp.where(bounds <= token, bounds, 0), axis=2)
    end = jnp.min(jnp.where(bounds > token, bounds, length), axis=2)
    first = start[:, ::rows] // rows
    last = (end[:, rows - 1 :: rows] - 1) // rows
    start = start[:, None, :]
    whole = pl.BlockSpec((blocks, rows, width), lambda b, s: (0, 0, 0))
    line = pl.BlockSpec((units, 1, rows), lambda b, s: (0, 0, b))
    full_line = pl.BlockSpec((units, 1, length), lambda b, s: (0, 0, 0))
    pairs = units * length * length // 4
    out, lse, delta = pl.pallas_call(
        partial(attend_kernel, units),
        grid_spec=pltpu.PrefetchScalarGridSpec(
            num_scalar_prefetch=1,
            grid=(blocks,),
            in_specs=[whole, line],
            out_specs=[
                pl.BlockSpec((1, rows, units * HEAD), lambda b, s: (b, 0, 0)),
                line,
                line,
            ],
        ),
        out_shape=[
            jax.ShapeDtypeStruct((blocks, rows, units * HEAD), jnp.bfloat16),
            jax.ShapeDtypeStruct((units, 1, length), jnp.float32),
            jax.ShapeDtypeStruct((units, 1, length), jnp.float32),
        ],
        compiler_params=pltpu.CompilerParams(vmem_limit_bytes=vmem_bytes),
        cost_estimate=pl.CostEstimate(
            flops=pairs * 4 * 256, bytes_accessed=units * length * 700, transcendentals=pairs
        ),
    )(first, packed, start)
    grads = pl.pallas_call(
        partial(attend_back_kernel, units),
        grid_spec=pltpu.PrefetchScalarGridSpec(
            num_scalar_prefetch=1,
            grid=(blocks,),
            in_specs=[whole, full_line, full_line, full_line],
            out_specs=pl.BlockSpec((1, rows, units * 3 * HEAD), lambda b, s: (b, 0, 0)),
            scratch_shapes=[pltpu.VMEM((units, blocks, rows, HEAD), jnp.float32)],
        ),
        out_shape=jax.ShapeDtypeStruct((blocks, rows, units * 3 * HEAD), jnp.bfloat16),
        compiler_params=pltpu.CompilerParams(vmem_limit_bytes=vmem_bytes),
        cost_estimate=pl.CostEstimate(
            flops=pairs * 10 * 256, bytes_accessed=units * length * 1000, transcendentals=pairs
        ),
    )(last, packed, start, lse, delta)
    return (out, grads)


def shards(
    hidden_in,
    cotangent,
    doc_lengths,
    norm1_gain,
    norm1_bias,
    norm2_gain,
    norm2_bias,
    qkv_weight,
    qkv_bias,
    out_weight,
    out_bias,
    fc1_weight,
    fc1_bias,
    fc2_weight,
):
    micros, tok_rows, width = hidden_in.shape
    heads = qkv_bias.shape[0]
    hidden_units = fc1_bias.shape[0]
    shard_rows = qkv_weight.shape[0]
    dp_count = lax.axis_size("dp")
    tokens = micros * tok_rows
    qkv_wide, att_wide = heads * 3 * HEAD, heads * HEAD
    unit_count = micros * heads
    units = -(-unit_count // dp_count)

    att_weights = lax.all_gather(
        jnp.concatenate(
            [qkv_weight.reshape(shard_rows, qkv_wide), out_weight.reshape(att_wide, shard_rows).T],
            axis=1,
        ),
        "dp",
        axis=0,
        tiled=True,
    )
    w_qkv, w_out = att_weights[:, :qkv_wide], att_weights[:, qkv_wide:]
    ff_weights = lax.all_gather(
        jnp.concatenate([fc1_weight, fc2_weight.T], axis=1), "dp", axis=0, tiled=True
    )
    w_up, w_down = ff_weights[:, :hidden_units], ff_weights[:, hidden_units:]

    query_index = lax.axis_index("dp") * tok_rows + jnp.arange(tok_rows, dtype=jnp.int32)
    position = jax.vmap(lambda lengths: documents(lengths, query_index)[1])(doc_lengths)
    cosine_table, sine_table = rotary_angles(position.reshape(tokens))
    hidden = hidden_in.reshape(tokens, width).astype(jnp.float32)
    grad_low = cotangent.reshape(tokens, width)
    centered = hidden - jnp.mean(hidden, axis=-1, keepdims=True)
    variance = jnp.mean(centered * centered, axis=-1, keepdims=True)
    inverse = lax.rsqrt(variance + norm_epsilon)
    unit_norm = centered * inverse
    first_low = (unit_norm * norm1_gain + norm1_bias).astype(jnp.bfloat16)
    second_low = (unit_norm * norm2_gain + norm2_bias).astype(jnp.bfloat16)

    def to_units(array):
        wide = array.shape[-1]
        array = array.reshape(micros, tok_rows, heads, wide).transpose(2, 0, 1, 3)
        array = array.reshape(unit_count, tok_rows, wide)
        if units * dp_count > unit_count:
            array = jnp.pad(array, ((0, units * dp_count - unit_count), (0, 0), (0, 0)))
        array = array.reshape(dp_count, units, tok_rows, wide).transpose(0, 2, 1, 3)
        array = array.reshape(dp_count, tok_rows, units * wide)
        return lax.all_to_all(array, "dp", split_axis=0, concat_axis=0, tiled=True)

    def from_units(array):
        wide = array.shape[-1] // units
        array = lax.all_to_all(array, "dp", split_axis=0, concat_axis=0, tiled=True)
        array = array.reshape(dp_count, tok_rows, units, wide).transpose(0, 2, 1, 3)
        array = array.reshape(units * dp_count, tok_rows, wide)
        array = array[:unit_count].reshape(heads, micros, tok_rows, wide)
        return array.transpose(1, 2, 0, 3).reshape(tokens, heads, wide)

    projected = (mul(first_low, w_qkv, NN) + qkv_bias.reshape(qkv_wide)).reshape(
        tokens, heads, 3 * HEAD
    )
    grad_att = mul(grad_low, w_out, NN).astype(jnp.bfloat16).reshape(tokens, heads, HEAD)
    packed = to_units(
        jnp.concatenate(
            [
                rotary(projected[..., :HEAD], cosine_table, sine_table).astype(jnp.bfloat16),
                rotary(projected[..., HEAD : 2 * HEAD], cosine_table, sine_table).astype(
                    jnp.bfloat16
                ),
                projected[..., 2 * HEAD :].astype(jnp.bfloat16),
                grad_att,
            ],
            axis=-1,
        )
    )
    up_proj = mul(second_low, w_up, NN) + fc1_bias
    activated, gelu_pull = jax.vjp(partial(jax.nn.gelu, approximate=False), up_proj)
    act_low = activated.astype(jnp.bfloat16)
    grad_up = gelu_pull(mul(grad_low, w_down, NN))[0].astype(jnp.bfloat16)
    grad_second = mul(grad_up, w_up, NT)
    ff_grads = jnp.concatenate(
        [
            mul(second_low, grad_up, TN).astype(jnp.bfloat16),
            mul(grad_low, act_low, TN).astype(jnp.bfloat16),
        ],
        axis=1,
    )
    down = mul(act_low, w_down, NT)
    packed, ff_grads, down, grad_second = lax.optimization_barrier(
        (packed, ff_grads, down, grad_second)
    )
    early = lax.psum_scatter(ff_grads, "dp", scatter_dimension=0, tiled=True).astype(jnp.float32)
    unit_ids = lax.axis_index("dp") * units + jnp.arange(units, dtype=jnp.int32)
    unit_out, unit_grads = attention(packed, doc_lengths[unit_ids % micros])
    attended = from_units(unit_out).reshape(tokens, att_wide)
    grad_parts = from_units(unit_grads)

    branches = lax.psum(
        (mul(attended, w_out, NT) + down).astype(jnp.bfloat16), "tensor"
    )
    layer_out = (hidden + branches.astype(jnp.float32) + out_bias).astype(jnp.bfloat16)

    grad_proj = jnp.concatenate(
        [
            rotary(grad_parts[..., :HEAD].astype(jnp.float32), cosine_table, -sine_table),
            rotary(
                grad_parts[..., HEAD : 2 * HEAD].astype(jnp.float32), cosine_table, -sine_table
            ),
            grad_parts[..., 2 * HEAD :].astype(jnp.float32),
        ],
        axis=-1,
    ).astype(jnp.bfloat16)
    grad_proj = grad_proj.reshape(tokens, qkv_wide)
    grad_first = mul(grad_proj, w_qkv, NT)
    grad_unit = (grad_first * norm1_gain + grad_second * norm2_gain).astype(jnp.bfloat16)
    grad_unit, branches_done = lax.optimization_barrier((grad_unit, layer_out))
    grad_unit = lax.psum(grad_unit, "tensor").astype(jnp.float32)
    late = lax.psum_scatter(
        jnp.concatenate(
            [
                mul(first_low, grad_proj, TN).astype(jnp.bfloat16),
                mul(grad_low, attended, TN).astype(jnp.bfloat16),
            ],
            axis=1,
        ),
        "dp", scatter_dimension=0, tiled=True
    ).astype(jnp.float32)
    grad_input = grad_low.astype(jnp.float32) + inverse * (
        grad_unit
        - jnp.mean(grad_unit, axis=-1, keepdims=True)
        - unit_norm * jnp.mean(grad_unit * unit_norm, axis=-1, keepdims=True)
    )
    mine = lax.axis_index("tensor")
    split = jnp.concatenate(
        [
            jnp.sum(grad_proj.astype(jnp.float32), axis=0),
            jnp.sum(grad_up.astype(jnp.float32), axis=0),
        ]
    )
    slots = jnp.arange(lax.axis_size("tensor"), dtype=jnp.int32)[:, None] == mine
    slots = jnp.where(slots, split[None, :], 0.0)
    sums = jnp.concatenate(
        [
            jnp.sum(grad_first * unit_norm, axis=0),
            jnp.sum(grad_first, axis=0),
            jnp.sum(grad_second * unit_norm, axis=0),
            jnp.sum(grad_second, axis=0),
            jnp.where(mine == 0, jnp.sum(grad_low.astype(jnp.float32), axis=0), 0.0),
            slots.reshape(-1),
        ]
    )
    sums = lax.psum(sums.reshape(-1, 128), ("dp", "tensor")).reshape(-1)
    norm_sums = sums[: 4 * width].reshape(4, width)
    grad_b_out = sums[4 * width : 5 * width]
    split = lax.dynamic_index_in_dim(sums[5 * width :].reshape(slots.shape), mine, 0, False)
    grad_b_qkv, grad_b_up = split[:qkv_wide], split[qkv_wide:]
    return (
        branches_done.reshape(hidden_in.shape),
        grad_input.astype(jnp.bfloat16).reshape(hidden_in.shape),
        norm_sums[0],
        norm_sums[1],
        norm_sums[2],
        norm_sums[3],
        late[:, :qkv_wide].reshape(shard_rows, heads, 3 * HEAD),
        grad_b_qkv.reshape(heads, 3 * HEAD),
        late[:, qkv_wide:].T.reshape(heads, HEAD, shard_rows),
        grad_b_out,
        early[:, :hidden_units],
        grad_b_up,
        early[:, hidden_units:].T,
    )


def solution(mesh):
    return jax.shard_map(
        shards,
        mesh=mesh,
        in_specs=(
            P(None, "dp", None),
            P(None, "dp", None),
            P(),
            P(),
            P(),
            P(),
            P(),
            P("dp", "tensor", None),
            P("tensor", None),
            P("tensor", None, "dp"),
            P(),
            P("dp", "tensor"),
            P("tensor"),
            P("tensor", "dp"),
        ),
        out_specs=(
            P(None, "dp", None),
            P(None, "dp", None),
            P(),
            P(),
            P(),
            P(),
            P("dp", "tensor", None),
            P("tensor", None),
            P("tensor", None, "dp"),
            P(),
            P("dp", "tensor"),
            P("tensor"),
            P("tensor", "dp"),
        ),
        check_vma=False,
    )
```
